1024 devices in a mesh: pipe: 32 (over y, z_hi, core), dp: 4 (over z_lo), head: 8 (over x).
Axes of the slice: x: 8, y: 8, z: 8 (z_hi: 2, z_lo: 4; z = z_hi * 4 + z_lo), core: 2. Of those that a mesh axis runs over, the one named last changes fastest.
Arguments:
- activations: bfloat16 [32, 2, 896, 8192], P('pipe', None, 'dp', 'head'), may hold values from -6 to 6
- out_grad: bfloat16 [32, 896, 8192], P('pipe', 'dp', 'head'), may hold values from -1.5 to 1.5
- key_grad: bfloat16 [32, 2, 896, 512], P('pipe', None, 'dp', 'head'), may hold values from -1.5 to 1.5
- key_weight: bfloat16 [32, 8192, 512], P('pipe', 'head'), may hold values from -0.25 to 0.25
- plan: int32 [32, 2], P('pipe'), may hold values from 0 to 1, each once within a row
- first_moment: bfloat16 [32, 8, 1024, 512], P('pipe', 'head', 'dp'), may hold values from -48 to 48
- second_moment: bfloat16 [32, 8, 1024, 512], P('pipe', 'head', 'dp'), may hold values from 10 to 300
Outputs:
- received_grad: bfloat16 [32, 896, 8192], P('pipe', 'dp', 'head')
- new_weight: bfloat16 [32, 8, 1024, 512], P('pipe', 'head', 'dp')
- new_first_moment: bfloat16 [32, 8, 1024, 512], P('pipe', 'head', 'dp')
- new_second_moment: bfloat16 [32, 8, 1024, 512], P('pipe', 'head', 'dp')
- checksum: float32 [32, 8, 4, 512], P('pipe', 'head', 'dp')
The draws below stay inside these ranges and needn't reach their ends.
Inputs may be any that keep to these rules, and one draw needn't show every extreme that they name: Each row of plan holds 0 and 1 once each.
All inputs are finite; a program needn't handle non-finite values.
Results may differ from the reference program's by a relative error of at most 0.0043.
Values may be sent and summed in bfloat16 or wider, within the bound.
A program may use at most 32 MiB of HBM per device.

```python
import math
import jax
import jax.numpy as jnp
from jax import lax

D = 8192
SECTIONS = 32
TOKENS = 896
KV_COLS = 512
GROUPS = 8
FEAT = 1024
N_DP = 4


def block_scale(rng, shape, pieces, smallest, largest):
    loudness = 1.0
    for dim, blocks in pieces:
        draws = jax.random.uniform(jax.random.fold_in(jax.random.fold_in(rng, 6), dim), (blocks,), jnp.float32, smallest / len(pieces), largest / len(pieces))
        loudness = loudness * jnp.repeat(jnp.exp(draws), shape[dim] // blocks).reshape((-1,) + (1,) * (len(shape) - 1 - dim))
    return loudness


def noise(rng, extent, deviation, bound, split=(), kind=jnp.bfloat16):
    array = jax.random.normal(rng, extent, jnp.float32) * deviation
    if len(split) > 0:
        array = block_scale(rng, extent, split, -0.22, 0.18) * array
    return jnp.clip(array, min=-bound, max=bound).astype(kind)


def setup_inputs(seed: int = 0) -> dict:
    key_of = jax.random.split(jax.random.key(seed), 8)
    activations = noise(key_of[0], (SECTIONS, 2, TOKENS, D), 1.0, 6.0, ((0, 32), (2, 4), (3, 8)))
    out_grad = noise(key_of[1], (SECTIONS, TOKENS, D), 0.25, 1.5, ((0, 32), (1, 4), (2, 8)))
    key_grad = noise(key_of[2], (SECTIONS, 2, TOKENS, KV_COLS), 0.25, 1.5, ((0, 32), (2, 4), (3, 8)))
    key_weight = noise(key_of[3], (SECTIONS, D, KV_COLS), KV_COLS ** -0.5, 0.25, ((0, 32), (1, 8)))
    plan = jax.vmap(lambda own: jax.random.permutation(own, 2))(jax.random.split(key_of[4], SECTIONS)).reshape((SECTIONS, 2)).astype(jnp.int32)
    first_moment = noise(key_of[5], (SECTIONS, GROUPS, FEAT, KV_COLS), 8.0, 48.0, ((0, 32), (1, 8), (2, 4)))
    second_moment = jnp.clip(jnp.exp(math.log(300.0) - 3.4011974 * jax.random.uniform(key_of[6], (SECTIONS, GROUPS, FEAT, KV_COLS), jnp.float32) ** block_scale(key_of[6], (SECTIONS, GROUPS, FEAT, KV_COLS), ((0, 32), (1, 8), (2, 4)), -0.2, 0.2)), 10.0, 300.0).astype(jnp.bfloat16)
    return {"activations": activations, "out_grad": out_grad, "key_grad": key_grad, "key_weight": key_weight, "plan": plan, "first_moment": first_moment, "second_moment": second_moment}


beta_one = 0.9
beta_two = 0.95
learn_rate = 0.01
weight_decay = 0.1
epsilon = 1e-08
first_fix = 1.0 - (0.9 ** 10) ** 10
second_fix = 1.0 - (0.95 ** 10) ** 10

def segment_grad(operands):
    incoming, key_rows, weight = operands
    added = jnp.dot(key_rows, weight.T, preferred_element_type=jnp.float32)
    return (incoming.astype(jnp.float32) + added).astype(jnp.bfloat16)

def update_section(operands):
    acts_here, keys_here, weight, first_old, second_old = operands
    gradient = jnp.einsum('mtf,mtc->fc', acts_here.astype(jnp.float32), keys_here.astype(jnp.float32), precision=lax.Precision.HIGHEST)
    gradient = gradient.reshape(GROUPS, FEAT, KV_COLS)
    old_weight = weight.astype(jnp.float32).reshape(GROUPS, FEAT, KV_COLS)
    first_fresh = beta_one * first_old.astype(jnp.float32) + (1.0 - beta_one) * gradient
    second_fresh = beta_two * second_old.astype(jnp.float32) + (1.0 - beta_two) * gradient * gradient
    update = first_fresh / first_fix / (jnp.sqrt(second_fresh / second_fix) + epsilon) + weight_decay * old_weight
    new_weight = (old_weight - learn_rate * update).astype(jnp.bfloat16)
    checksum = lax.optimization_barrier(jnp.mean(gradient.reshape(GROUPS, N_DP, FEAT // N_DP, KV_COLS), axis=2))
    return (new_weight, first_fresh.astype(jnp.bfloat16), second_fresh.astype(jnp.bfloat16), checksum)

def reference(activations, out_grad, key_grad, key_weight, plan, first_moment, second_moment):
    early_index = plan[:, 0].astype(jnp.int32)[:, None, None, None]
    late_index = plan[:, 1].astype(jnp.int32)[:, None, None, None]
    early_keys = jnp.take_along_axis(key_grad, early_index, axis=1)[:, 0]
    late_keys = jnp.take_along_axis(key_grad, late_index, axis=1)[:, 0]
    first_pass = lax.map(segment_grad, (out_grad, early_keys, key_weight))
    received = jnp.roll(first_pass, -1, axis=0)
    second_pass = lax.map(segment_grad, (received, late_keys, key_weight))
    received_grad = jnp.roll(second_pass, -1, axis=0)
    new_weight, new_first, new_second, checksum = lax.map(update_section, (activations, key_grad, key_weight, first_moment, second_moment))
    return (received_grad, new_weight, new_first, new_second, checksum)
```

```python
import functools

import jax
import jax.numpy as jnp
from jax import lax
from jax.experimental import pallas as pl
from jax.experimental.pallas import tpu as pltpu
from jax.sharding import PartitionSpec as P

MESH = pl.DeviceIdType.MESH
beta_one = 0.9
beta_two = 0.95
learn_rate = 0.01
weight_decay = 0.1
epsilon = 1e-08
first_fix = 1.0 - (0.9**10) ** 10
second_fix = 1.0 - (0.95**10) ** 10

HEADS = 8
N_DP = 4
ROWS = 224
COLS = 512
HEAD_COLS = COLS // HEADS
SHARD = 256
CHUNKS = 4
WIDE = 256
SLAB = 32


def nt(lhs, rhs):
    return lax.dot_general(lhs, rhs, (((1,), (1,)), ((), ())), preferred_element_type=jnp.float32)


def tn(lhs, rhs):
    return lax.dot_general(lhs, rhs, (((0,), (0,)), ((), ())), preferred_element_type=jnp.float32)


def kernel(
    plan, kg, act, og, w, m1, m2,
    out_r, out_w, out_m1, out_m2, out_c,
    kgv, kt, ket, early, late, kn, ke, actv, ogv, wv, m1v, m2v,
    fp, r1, sp, pb, ab, ob, gf, owv, om1v, om2v, ocv,
    load_sem, key_send, key_recv, act_send, act_recv, end_send, end_recv,
    fp_send, fp_recv, sp_send, sp_recv, ob_send, ob_recv, store_sem,
):
    pipe, dp, head = lax.axis_index("pipe"), lax.axis_index("dp"), lax.axis_index("head")
    n_pipe = lax.axis_size("pipe")
    ahead = (lax.rem(pipe + n_pipe - 1, n_pipe), dp, head)
    behind = (lax.rem(pipe + 1, n_pipe), dp, head)
    is_inner = jnp.logical_or(dp == 1, dp == 2)
    is_end = jnp.logical_not(is_inner)
    low = dp < 2
    my_end = jnp.where(low, 0, 3)
    my_inner = jnp.where(low, 1, 2)
    other_inner = jnp.where(low, 2, 1)
    other_end = jnp.where(low, 3, 0)
    even = lax.rem(pipe, 2) == 0

    def peer(step):
        return (pipe, dp, lax.rem(head + step, HEADS))

    def remote(src, dst, send, recv, device):
        return pltpu.make_async_remote_copy(
            src_ref=src, dst_ref=dst, send_sem=send, recv_sem=recv, device_id=device, device_id_type=MESH
        )

    def load(k, src, dst):
        copy = pltpu.make_async_copy(src, dst, load_sem.at[k])
        copy.start()
        return copy

    kg_in = load(0, kg, kgv)
    barrier = pltpu.get_barrier_semaphore()
    greeted = [peer(d) for d in range(1, HEADS)]
    greeted += [(pipe, lax.rem(dp + d, N_DP), head) for d in range(1, N_DP)]
    greeted += [ahead, behind]
    for device in greeted:
        pl.semaphore_signal(barrier, inc=1, device_id=device, device_id_type=MESH)
    act_in = [
        load(1 + 2 * j + m, act.at[m, :, pl.ds(WIDE * j, WIDE)], actv.at[j, pl.ds(ROWS * m, ROWS)])
        for j in range(CHUNKS)
        for m in range(2)
    ]
    w_in = load(9, w, wv)
    og_in = [load(10 + j, og.at[:, pl.ds(WIDE * j, WIDE)], ogv.at[j]) for j in range(CHUNKS)]
    m1_in = load(14, m1, m1v)
    m2_in = load(15, m2, m2v)

    kg_in.wait()
    swap = jnp.full((HEAD_COLS, ROWS), plan[0, 0], jnp.int32) != 0
    zero, one = kgv[0].astype(jnp.float32), kgv[1].astype(jnp.float32)
    kt[0, head] = jnp.where(swap, one, zero).astype(jnp.bfloat16)
    kt[1, head] = jnp.where(swap, zero, one).astype(jnp.bfloat16)
    pl.semaphore_wait(barrier, len(greeted))

    def key_copy(which, d):
        return remote(
            kt.at[which, head], kt.at[which, head], key_send.at[which, d - 1], key_recv.at[which, d - 1], peer(d)
        )

    def end_key_copy(d):
        return remote(ket.at[head], ket.at[head], key_send.at[2, d - 1], key_recv.at[2, d - 1], peer(d))

    order = (4, 3, 5, 2, 6, 1, 7)
    for d in order:
        key_copy(0, d).start()
    for copy in act_in:
        copy.wait()

    targets = (other_end, other_inner, my_inner)
    act_copies = [
        remote(actv.at[targets[k]], ab.at[k], act_send.at[k], act_recv.at[k], (pipe, my_inner, head))
        for k in range(3)
    ]
    end_block = remote(kgv, ket.at[head], end_send, end_recv, (pipe, my_inner, head))

    @pl.when(is_end)
    def _():
        act_copies[0].start()
        end_block.start()

    for d in order:
        key_copy(1, d).start()

    @pl.when(is_end)
    def _():
        act_copies[1].start()
        act_copies[2].start()

    w_in.wait()
    for copy in og_in:
        copy.wait()
    for d in order[::-1]:
        key_copy(0, d).wait_recv()
    early[...] = kt[0].reshape(COLS, ROWS).T

    def fp_copy(j):
        return remote(fp.at[j], r1.at[j], fp_send.at[j], fp_recv.at[j], ahead)

    def sp_copy(j):
        return remote(sp.at[j], out_r.at[:, pl.ds(WIDE * j, WIDE)], sp_send.at[j], sp_recv.at[j], ahead)

    for j in range(CHUNKS):
        added = nt(early[...], wv[WIDE * j : WIDE * (j + 1), :])
        fp[j] = (ogv[j].astype(jnp.float32) + added).astype(jnp.bfloat16)
        fp_copy(j).start()

    @pl.when(is_inner)
    def _():
        end_block.wait_recv()
        for d in order:
            end_key_copy(d).start()

    for d in order[::-1]:
        key_copy(1, d).wait_recv()
    late[...] = kt[1].reshape(COLS, ROWS).T
    swap_all = jnp.full((ROWS, COLS), plan[0, 0], jnp.int32) != 0
    zero, one = early[...].astype(jnp.float32), late[...].astype(jnp.float32)
    kn[:ROWS] = jnp.where(swap_all, one, zero).astype(jnp.bfloat16)
    kn[ROWS:] = jnp.where(swap_all, zero, one).astype(jnp.bfloat16)

    to_end = remote(pb.at[2], ob.at[1], ob_send.at[2], ob_recv.at[1], (pipe, my_end, head))
    to_far = remote(pb.at[0], ob.at[0], ob_send.at[0], ob_recv.at[0], (pipe, other_end, head))
    to_near = remote(pb.at[1], ob.at[0], ob_send.at[1], ob_recv.at[0], (pipe, other_inner, head))

    @pl.when(is_inner)
    def _():
        pb[2] = tn(actv[my_end], kn[...]).astype(jnp.bfloat16)
        to_end.start()

    @pl.when(is_end)
    def _():
        gf[...] = tn(actv[dp], kn[...])

    def second(j):
        fp_copy(j).wait_recv()
        added = nt(late[...], wv[WIDE * j : WIDE * (j + 1), :])
        sp[j] = (r1[j].astype(jnp.float32) + added).astype(jnp.bfloat16)
        sp_copy(j).start()

    @pl.when(even)
    def _():
        for j in range(CHUNKS):
            second(j)

    def pair(k):
        act_copies[k].wait_recv()
        return tn(actv[targets[k]], kn[...]) + tn(ab[k], ke[...])

    @pl.when(is_inner)
    def _():
        for d in order[::-1]:
            end_key_copy(d).wait_recv()
        for m in range(2):
            for h in range(0, HEADS, 2):
                both = jnp.concatenate([ket[h, m], ket[h + 1, m]], axis=0)
                ke[ROWS * m : ROWS * (m + 1), HEAD_COLS * h : HEAD_COLS * (h + 2)] = both.T
        pb[0] = pair(0).astype(jnp.bfloat16)
        to_far.start()
        pb[1] = pair(1).astype(jnp.bfloat16)
        to_near.start()

    @pl.when(jnp.logical_not(even))
    def _():
        for j in range(CHUNKS):
            second(j)

    @pl.when(is_inner)
    def _():
        gf[...] = pair(2)

    m1_in.wait()
    m2_in.wait()
    to_far.wait_recv()

    @pl.when(is_end)
    def _():
        to_end.wait_recv()
        gf[...] = gf[...] + ob[1].astype(jnp.float32)

    def slab(i, total):
        rows = pl.ds(pl.multiple_of(i * SLAB, SLAB), SLAB)
        gradient = gf[rows, :] + ob[0, rows, :].astype(jnp.float32)
        old_weight = wv[pl.ds(pl.multiple_of(dp * SHARD + i * SLAB, SLAB), SLAB), :].astype(jnp.float32)
        first_fresh = beta_one * m1v[rows, :].astype(jnp.float32) + (1.0 - beta_one) * gradient
        second_fresh = beta_two * m2v[rows, :].astype(jnp.float32) + (1.0 - beta_two) * gradient * gradient
        update = (
            first_fresh / first_fix / (jnp.sqrt(second_fresh / second_fix) + epsilon)
            + weight_decay * old_weight
        )
        owv[rows, :] = (old_weight - learn_rate * update).astype(jnp.bfloat16)
        om1v[rows, :] = first_fresh.astype(jnp.bfloat16)
        om2v[rows, :] = second_fresh.astype(jnp.bfloat16)
        return total + jnp.sum(gradient, axis=0, keepdims=True)

    total = lax.fori_loop(0, SHARD // SLAB, slab, jnp.zeros((1, COLS), jnp.float32))
    ocv[...] = total / SHARD
    stores = [(owv, out_w), (om1v, out_m1), (om2v, out_m2), (ocv, out_c)]
    stores = [pltpu.make_async_copy(src, dst, store_sem.at[k]) for k, (src, dst) in enumerate(stores)]
    for copy in stores:
        copy.start()

    for j in range(CHUNKS):
        sp_copy(j).wait_recv()
    for j in range(CHUNKS):
        fp_copy(j).wait_send()
        sp_copy(j).wait_send()
    for d in order:
        key_copy(0, d).wait_send()
        key_copy(1, d).wait_send()

    @pl.when(is_end)
    def _():
        for copy in act_copies:
            copy.wait_send()
        end_block.wait_send()

    @pl.when(is_inner)
    def _():
        for d in order:
            end_key_copy(d).wait_send()
        to_end.wait_send()
        to_far.wait_send()
        to_near.wait_send()

    for copy in stores:
        copy.wait()


def body(activations, out_grad, key_grad, key_weight, plan, first_moment, second_moment):
    keys = jnp.swapaxes(key_grad[0], 1, 2)
    bf16, f32 = jnp.bfloat16, jnp.float32
    vmem = pltpu.VMEM
    dma = pltpu.SemaphoreType.DMA
    shard = jax.ShapeDtypeStruct((SHARD, COLS), bf16)
    anywhere = pl.BlockSpec(memory_space=pl.ANY)
    outs = pl.pallas_call(
        kernel,
        out_shape=(
            jax.ShapeDtypeStruct((ROWS, CHUNKS * WIDE), bf16),
            shard, shard, shard,
            jax.ShapeDtypeStruct((1, COLS), f32),
        ),
        in_specs=[pl.BlockSpec(memory_space=pltpu.SMEM)] + [anywhere] * 6,
        out_specs=[anywhere] * 5,
        scratch_shapes=[
            vmem((2, HEAD_COLS, ROWS), bf16),
            vmem((2, HEADS, HEAD_COLS, ROWS), bf16),
            vmem((HEADS, 2, HEAD_COLS, ROWS), bf16),
            vmem((ROWS, COLS), bf16),
            vmem((ROWS, COLS), bf16),
            vmem((2 * ROWS, COLS), bf16),
            vmem((2 * ROWS, COLS), bf16),
            vmem((CHUNKS, 2 * ROWS, WIDE), bf16),
            vmem((CHUNKS, ROWS, WIDE), bf16),
            vmem((CHUNKS * WIDE, COLS), bf16),
            vmem((SHARD, COLS), bf16),
            vmem((SHARD, COLS), bf16),
            vmem((CHUNKS, ROWS, WIDE), bf16),
            vmem((CHUNKS, ROWS, WIDE), bf16),
            vmem((CHUNKS, ROWS, WIDE), bf16),
            vmem((3, SHARD, COLS), bf16),
            vmem((3, 2 * ROWS, WIDE), bf16),
            vmem((2, SHARD, COLS), bf16),
            vmem((SHARD, COLS), f32),
            vmem((SHARD, COLS), bf16),
            vmem((SHARD, COLS), bf16),
            vmem((SHARD, COLS), bf16),
            vmem((1, COLS), f32),
            dma((16,)),
            dma((3, HEADS - 1)), dma((3, HEADS - 1)),
            dma((3,)), dma((3,)),
            dma, dma,
            dma((CHUNKS,)), dma((CHUNKS,)),
            dma((CHUNKS,)), dma((CHUNKS,)),
            dma((3,)), dma((2,)),
            dma((4,)),
        ],
        compiler_params=pltpu.CompilerParams(
            collective_id=0, has_side_effects=True, vmem_limit_bytes=40 << 20
        ),
        cost_estimate=pl.CostEstimate(flops=1_400_000_000, bytes_accessed=5_000_000, transcendentals=131_072),
    )(plan, keys, activations[0], out_grad[0], key_weight[0], first_moment[0, 0], second_moment[0, 0])
    passed, new_weight, new_first, new_second, checksum = outs
    return passed[None], new_weight[None, None], new_first[None, None], new_second[None, None], checksum[None, None]


def solution(mesh):
    return jax.shard_map(
        body,
        mesh=mesh,
        in_specs=(
            P("pipe", None, "dp", "head"),
            P("pipe", "dp", "head"),
            P("pipe", None, "dp", "head"),
            P("pipe", "head", None),
            P("pipe", None),
            P("pipe", "head", "dp", None),
            P("pipe", "head", "dp", None),
        ),
        out_specs=(
            P("pipe", "dp", "head"),
            P("pipe", "head", "dp", None),
            P("pipe", "head", "dp", None),
            P("pipe", "head", "dp", None),
            P("pipe", "head", "dp", None),
        ),
        check_vma=False,
    )
```

```python
import functools

import jax
import jax.numpy as jnp
from jax import lax
from jax.experimental import pallas as pl
from jax.experimental.pallas import tpu as pltpu
from jax.sharding import PartitionSpec as P

MESH = pl.DeviceIdType.MESH
beta_one = 0.9
beta_two = 0.95
learn_rate = 0.01
weight_decay = 0.1
epsilon = 1e-08
first_fix = 1.0 - (0.9**10) ** 10
second_fix = 1.0 - (0.95**10) ** 10

HEADS = 8
N_DP = 4
ROWS = 224
COLS = 512
HEAD_COLS = COLS // HEADS
SHARD = 256
FEAT = 1024
TOKEN_PARTS = ((0, 128), (128, 96))
WIDE = 512
CHUNKS = [(part, half) for part in range(2) for half in range(2)]
SLAB = 32


def nt(lhs, rhs):
    return lax.dot_general(lhs, rhs, (((1,), (1,)), ((), ())), preferred_element_type=jnp.float32)


def tn(lhs, rhs):
    return lax.dot_general(lhs, rhs, (((0,), (0,)), ((), ())), preferred_element_type=jnp.float32)


def kernel(
    plan, kg, act, og, w, m1, m2,
    out_r, out_w, out_m1, out_m2, out_c,
    kgv, kta, ktb, ktl, ket, early, late, kn, ke, actv, oga, ogb, wv, m1v, m2v,
    fpa, fpb, r1a, r1b, spa, spb, pb, ab, ob, gf, owv, om1v, om2v, ocv,
    planv, load_sem, key_send, key_recv, act_send, act_recv, end_send, end_recv,
    fp_send, fp_recv, sp_send, sp_recv, ob_send, ob_recv, store_sem,
):
    pipe, dp, head = lax.axis_index("pipe"), lax.axis_index("dp"), lax.axis_index("head")
    n_pipe = lax.axis_size("pipe")
    ahead = (lax.rem(pipe + n_pipe - 1, n_pipe), dp, head)
    behind = (lax.rem(pipe + 1, n_pipe), dp, head)
    is_inner = jnp.logical_or(dp == 1, dp == 2)
    is_end = jnp.logical_not(is_inner)
    low = dp < 2
    my_end = jnp.where(low, 0, 3)
    my_inner = jnp.where(low, 1, 2)
    other_inner = jnp.where(low, 2, 1)
    other_end = jnp.where(low, 3, 0)
    even = lax.rem(pipe, 2) == 0

    def peer(step):
        return (pipe, dp, lax.rem(head + step, HEADS))

    def remote(src, dst, send, recv, device):
        return pltpu.make_async_remote_copy(
            src_ref=src, dst_ref=dst, send_sem=send, recv_sem=recv, device_id=device, device_id_type=MESH
        )

    def load(k, src, dst):
        copy = pltpu.make_async_copy(src, dst, load_sem.at[k])
        copy.start()
        return copy

    plan_in = load(16, plan, planv)
    kg_in = load(0, kg, kgv)
    barrier = pltpu.get_barrier_semaphore()
    greeted = [peer(d) for d in range(1, HEADS)]
    greeted += [(pipe, lax.rem(dp + d, N_DP), head) for d in range(1, N_DP)]
    greeted += [ahead, behind]
    for device in greeted:
        pl.semaphore_signal(barrier, inc=1, device_id=device, device_id_type=MESH)
    act_in = [
        load(1 + 2 * j + m, act.at[m, :, pl.ds(SHARD * j, SHARD)], actv.at[j, pl.ds(ROWS * m, ROWS)])
        for j in range(N_DP)
        for m in range(2)
    ]
    w_in = load(9, w, wv)
    ogv, fp, r1, sp = (oga, ogb), (fpa, fpb), (r1a, r1b), (spa, spb)
    og_in = [
        load(10 + j, og.at[pl.ds(*TOKEN_PARTS[part]), pl.ds(WIDE * half, WIDE)], ogv[part].at[half])
        for j, (part, half) in enumerate(CHUNKS)
    ]
    m1_in = load(14, m1, m1v)
    m2_in = load(15, m2, m2v)

    plan_in.wait()
    kg_in.wait()
    swap = jnp.full((HEAD_COLS, ROWS), planv[0, 0], jnp.int32) != 0
    zero, one = kgv[0].astype(jnp.float32), kgv[1].astype(jnp.float32)
    first = jnp.where(swap, one, zero).astype(jnp.bfloat16)
    kta[head] = first[:, : TOKEN_PARTS[0][1]]
    ktb[head] = first[:, TOKEN_PARTS[0][1] :]
    ktl[head] = jnp.where(swap, zero, one).astype(jnp.bfloat16)
    pl.semaphore_wait(barrier, len(greeted))

    early_parts = (kta, ktb)

    def early_copy(part, d):
        block = early_parts[part].at[head]
        return remote(block, block, key_send.at[part, d - 1], key_recv.at[part, d - 1], peer(d))

    def passed_on(blocks, row, d, via_below):
        if d in (1, 2, 6, 7):
            owner, device = head, peer(d)
        elif d == 3 or (d == 4 and via_below):
            owner, device = lax.rem(head + HEADS - 2, HEADS), peer(d - 2)
        else:
            owner, device = lax.rem(head + 2, HEADS), peer(d + 2)
        block = blocks.at[owner]
        return remote(block, block, key_send.at[row, d - 1], key_recv.at[row, d - 1], device)

    def late_copy(d):
        return passed_on(ktl, 2, d, True)

    def end_key_copy(d):
        return passed_on(ket, 3, d, False)

    far, near = (4, 3, 5, 2, 6, 1, 7), (2, 6, 1, 7)
    for part in range(2):
        for d in far:
            early_copy(part, d).start()
    for copy in act_in:
        copy.wait()

    targets = (other_end, other_inner, my_inner)
    act_copies = [
        remote(actv.at[targets[k]], ab.at[k], act_send.at[k], act_recv.at[k], (pipe, my_inner, head))
        for k in range(3)
    ]
    end_block = remote(kgv, ket.at[head], end_send, end_recv, (pipe, my_inner, head))

    @pl.when(is_end)
    def _():
        end_block.start()
        act_copies[0].start()

    for d in near:
        late_copy(d).start()

    def fp_copy(j):
        part, half = CHUNKS[j]
        return remote(fp[part].at[half], r1[part].at[half], fp_send.at[j], fp_recv.at[j], ahead)

    def sp_copy(j):
        part, half = CHUNKS[j]
        place = out_r.at[pl.ds(*TOKEN_PARTS[part]), pl.ds(WIDE * half, WIDE)]
        return remote(sp[part].at[half], place, sp_send.at[j], sp_recv.at[j], ahead)

    def first(j):
        part, half = CHUNKS[j]
        start, rows = TOKEN_PARTS[part]
        added = nt(early[start : start + rows, :], wv[WIDE * half : WIDE * (half + 1), :])
        fp[part][half] = (ogv[part][half].astype(jnp.float32) + added).astype(jnp.bfloat16)
        fp_copy(j).start()

    w_in.wait()
    for copy in og_in:
        copy.wait()
    for part, (start, rows) in enumerate(TOKEN_PARTS):
        for d in far[::-1]:
            early_copy(part, d).wait_recv()
        early[start : start + rows, :] = early_parts[part][...].reshape(COLS, rows).T
        for j in range(len(CHUNKS)):
            if CHUNKS[j][0] == part:
                first(j)
        if part == 0:

            @pl.when(is_inner)
            def _():
                end_block.wait_recv()
                for d in near:
                    end_key_copy(d).start()

    late_copy(2).wait_recv()
    late_copy(3).start()
    late_copy(4).start()
    late_copy(6).wait_recv()
    late_copy(5).start()

    @pl.when(is_inner)
    def _():
        end_key_copy(2).wait_recv()
        end_key_copy(3).start()
        end_key_copy(6).wait_recv()
        end_key_copy(4).start()
        end_key_copy(5).start()

    for d in (1, 7, 5, 3, 4):
        late_copy(d).wait_recv()
    late[...] = ktl[...].reshape(COLS, ROWS).T
    swap_all = jnp.full((ROWS, COLS), planv[0, 0], jnp.int32) != 0
    zero, one = early[...].astype(jnp.float32), late[...].astype(jnp.float32)
    kn[:ROWS] = jnp.where(swap_all, one, zero).astype(jnp.bfloat16)
    kn[ROWS:] = jnp.where(swap_all, zero, one).astype(jnp.bfloat16)

    to_end = remote(pb.at[2], ob.at[1], ob_send.at[2], ob_recv.at[1], (pipe, my_end, head))
    to_far = remote(pb.at[0], ob.at[0], ob_send.at[0], ob_recv.at[0], (pipe, other_end, head))
    to_near = remote(pb.at[1], ob.at[0], ob_send.at[1], ob_recv.at[0], (pipe, other_inner, head))

    def second(j):
        part, half = CHUNKS[j]
        start, rows = TOKEN_PARTS[part]
        fp_copy(j).wait_recv()
        added = nt(late[start : start + rows, :], wv[WIDE * half : WIDE * (half + 1), :])
        sp[part][half] = (r1[part][half].astype(jnp.float32) + added).astype(jnp.bfloat16)
        sp_copy(j).start()

    @pl.when(is_end)
    def _():
        act_copies[1].start()

    @pl.when(even)
    def _():
        for j in range(len(CHUNKS)):
            second(j)

    @pl.when(is_inner)
    def _():
        pb[2] = tn(actv[my_end], kn[...]).astype(jnp.bfloat16)
        to_end.start()

    @pl.when(is_end)
    def _():
        gf[...] = tn(actv[dp], kn[...])

    def pair(k):
        act_copies[k].wait_recv()
        return tn(actv[targets[k]], kn[...]) + tn(ab[k], ke[...])

    @pl.when(is_inner)
    def _():
        for d in (1, 7, 3, 5, 4):
            end_key_copy(d).wait_recv()
        for m in range(2):
            for h in range(0, HEADS, 2):
                both = jnp.concatenate([ket[h, m], ket[h + 1, m]], axis=0)
                ke[ROWS * m : ROWS * (m + 1), HEAD_COLS * h : HEAD_COLS * (h + 2)] = both.T
        pb[0] = pair(0).astype(jnp.bfloat16)
        to_far.start()

    @pl.when(jnp.logical_not(even))
    def _():
        for j in range(len(CHUNKS)):
            second(j)

    @pl.when(is_end)
    def _():
        act_copies[1].wait_send()
        act_copies[2].start()

    @pl.when(is_inner)
    def _():
        pb[1] = pair(1).astype(jnp.bfloat16)
        to_near.start()
        gf[...] = pair(2)

    m1_in.wait()
    m2_in.wait()
    to_far.wait_recv()

    @pl.when(is_end)
    def _():
        to_end.wait_recv()
        gf[...] = gf[...] + ob[1].astype(jnp.float32)

    def slab(i, total):
        rows = pl.ds(pl.multiple_of(i * SLAB, SLAB), SLAB)
        gradient = gf[rows, :] + ob[0, rows, :].astype(jnp.float32)
        old_weight = wv[pl.ds(pl.multiple_of(dp * SHARD + i * SLAB, SLAB), SLAB), :].astype(jnp.float32)
        first_fresh = beta_one * m1v[rows, :].astype(jnp.float32) + (1.0 - beta_one) * gradient
        second_fresh = beta_two * m2v[rows, :].astype(jnp.float32) + (1.0 - beta_two) * gradient * gradient
        update = (
            first_fresh / first_fix / (jnp.sqrt(second_fresh / second_fix) + epsilon)
            + weight_decay * old_weight
        )
        owv[rows, :] = (old_weight - learn_rate * update).astype(jnp.bfloat16)
        om1v[rows, :] = first_fresh.astype(jnp.bfloat16)
        om2v[rows, :] = second_fresh.astype(jnp.bfloat16)
        return total + jnp.sum(gradient, axis=0, keepdims=True)

    total = lax.fori_loop(0, SHARD // SLAB, slab, jnp.zeros((1, COLS), jnp.float32))
    ocv[...] = total / SHARD
    stores = [(owv, out_w), (om1v, out_m1), (om2v, out_m2), (ocv, out_c)]
    stores = [pltpu.make_async_copy(src, dst, store_sem.at[k]) for k, (src, dst) in enumerate(stores)]
    for copy in stores:
        copy.start()

    for j in range(len(CHUNKS)):
        sp_copy(j).wait_recv()
    for j in range(len(CHUNKS)):
        fp_copy(j).wait_send()
        sp_copy(j).wait_send()
    for d in far:
        early_copy(0, d).wait_send()
        early_copy(1, d).wait_send()
        late_copy(d).wait_send()

    @pl.when(is_end)
    def _():
        act_copies[0].wait_send()
        act_copies[2].wait_send()
        end_block.wait_send()

    @pl.when(is_inner)
    def _():
        for d in far:
            end_key_copy(d).wait_send()
        to_end.wait_send()
        to_far.wait_send()
        to_near.wait_send()

    for copy in stores:
        copy.wait()


def hand_over(*refs):
    count = (len(refs) - 1) // 2
    sems = refs[-1]
    copies = [pltpu.make_async_copy(refs[k], refs[count + k], sems.at[k]) for k in range(count)]
    for copy in copies:
        copy.start()
    for copy in copies:
        copy.wait()


def body(activations, out_grad, key_grad, key_weight, plan, first_moment, second_moment):
    keys = jnp.swapaxes(key_grad[0], 1, 2)
    bf16, f32 = jnp.bfloat16, jnp.float32
    vmem = pltpu.VMEM
    dma = pltpu.SemaphoreType.DMA
    shard = jax.ShapeDtypeStruct((SHARD, COLS), bf16)
    anywhere = pl.BlockSpec(memory_space=pl.ANY)
    hbm = pl.BlockSpec(memory_space=pltpu.HBM)
    outs = pl.pallas_call(
        kernel,
        out_shape=(
            jax.ShapeDtypeStruct((ROWS, FEAT), bf16),
            shard, shard, shard,
            jax.ShapeDtypeStruct((1, COLS), f32),
        ),
        in_specs=[hbm] * 7,
        out_specs=[anywhere] * 5,
        scratch_shapes=[
            vmem((2, HEAD_COLS, ROWS), bf16),
            vmem((HEADS, HEAD_COLS, TOKEN_PARTS[0][1]), bf16),
            vmem((HEADS, HEAD_COLS, TOKEN_PARTS[1][1]), bf16),
            vmem((HEADS, HEAD_COLS, ROWS), bf16),
            vmem((HEADS, 2, HEAD_COLS, ROWS), bf16),
            vmem((ROWS, COLS), bf16),
            vmem((ROWS, COLS), bf16),
            vmem((2 * ROWS, COLS), bf16),
            vmem((2 * ROWS, COLS), bf16),
            vmem((N_DP, 2 * ROWS, SHARD), bf16),
            vmem((2, TOKEN_PARTS[0][1], WIDE), bf16),
            vmem((2, TOKEN_PARTS[1][1], WIDE), bf16),
            vmem((FEAT, COLS), bf16),
            vmem((SHARD, COLS), bf16),
            vmem((SHARD, COLS), bf16),
            vmem((2, TOKEN_PARTS[0][1], WIDE), bf16),
            vmem((2, TOKEN_PARTS[1][1], WIDE), bf16),
            vmem((2, TOKEN_PARTS[0][1], WIDE), bf16),
            vmem((2, TOKEN_PARTS[1][1], WIDE), bf16),
            vmem((2, TOKEN_PARTS[0][1], WIDE), bf16),
            vmem((2, TOKEN_PARTS[1][1], WIDE), bf16),
            vmem((3, SHARD, COLS), bf16),
            vmem((3, 2 * ROWS, SHARD), bf16),
            vmem((2, SHARD, COLS), bf16),
            vmem((SHARD, COLS), f32),
            vmem((SHARD, COLS), bf16),
            vmem((SHARD, COLS), bf16),
            vmem((SHARD, COLS), bf16),
            vmem((1, COLS), f32),
            pltpu.SMEM((1, 2), jnp.int32),
            dma((17,)),
            dma((4, HEADS - 1)), dma((4, HEADS - 1)),
            dma((3,)), dma((3,)),
            dma, dma,
            dma((len(CHUNKS),)), dma((len(CHUNKS),)),
            dma((len(CHUNKS),)), dma((len(CHUNKS),)),
            dma((3,)), dma((2,)),
            dma((4,)),
        ],
        compiler_params=pltpu.CompilerParams(
            collective_id=0, has_side_effects=True, vmem_limit_bytes=40 << 20
        ),
        cost_estimate=pl.CostEstimate(flops=1_400_000_000, bytes_accessed=5_000_000, transcendentals=131_072),
    )(*[pltpu.with_memory_space_constraint(v, pltpu.HBM) for v in (plan, keys, activations[0], out_grad[0], key_weight[0], first_moment[0, 0], second_moment[0, 0])])
    outs = pl.pallas_call(
        hand_over,
        out_shape=tuple(jax.ShapeDtypeStruct(value.shape, value.dtype) for value in outs),
        in_specs=[anywhere] * len(outs),
        out_specs=[hbm] * len(outs),
        scratch_shapes=[dma((len(outs),))],
        compiler_params=pltpu.CompilerParams(vmem_limit_bytes=1 << 20),
    )(*outs)
    passed, new_weight, new_first, new_second, checksum = outs
    return passed[None], new_weight[None, None], new_first[None, None], new_second[None, None], checksum[None, None]


def solution(mesh):
    return jax.shard_map(
        body,
        mesh=mesh,
        in_specs=(
            P("pipe", None, "dp", "head"),
            P("pipe", "dp", "head"),
            P("pipe", None, "dp", "head"),
            P("pipe", "head", None),
            P("pipe", None),
            P("pipe", "head", "dp", None),
            P("pipe", "head", "dp", None),
        ),
        out_specs=(
            P("pipe", "dp", "head"),
            P("pipe", "head", "dp", None),
            P("pipe", "head", "dp", None),
            P("pipe", "head", "dp", None),
            P("pipe", "head", "dp", None),
        ),
        check_vma=False,
    )
```

```python
import functools

import jax
import jax.numpy as jnp
from jax import lax
from jax.experimental import pallas as pl
from jax.experimental.pallas import tpu as pltpu
from jax.sharding import PartitionSpec as P

MESH = pl.DeviceIdType.MESH
beta_one = 0.9
beta_two = 0.95
learn_rate = 0.01
weight_decay = 0.1
epsilon = 1e-08
first_fix = 1.0 - (0.9**10) ** 10
second_fix = 1.0 - (0.95**10) ** 10

HEADS = 8
N_DP = 4
ROWS = 224
COLS = 512
HEAD_COLS = COLS // HEADS
SHARD = 256
FEAT = 1024
TOKEN_PARTS = ((0, 128), (128, 96))
WIDE = 512
CHUNKS = [(part, half) for part in range(2) for half in range(2)]
SLAB = 32


def nt(lhs, rhs):
    return lax.dot_general(lhs, rhs, (((1,), (1,)), ((), ())), preferred_element_type=jnp.float32)


def tn(lhs, rhs):
    return lax.dot_general(lhs, rhs, (((0,), (0,)), ((), ())), preferred_element_type=jnp.float32)


def kernel(
    plan, kg, act, og, w, m1, m2,
    out_r, out_w, out_m1, out_m2, out_c,
    kgv, kta, ktb, ktl, ket, early, late, kn, ke, actv, oga, ogb, wv, m1v, m2v,
    fpa, fpb, r1a, r1b, spa, spb, pb, ab, own, ob, gf, owv, om1v, om2v, ocv,
    planv, load_sem, key_send, key_recv, act_send, act_recv, end_send, end_recv,
    fp_send, fp_recv, sp_send, sp_recv, ob_send, ob_recv, store_sem,
):
    pipe, dp, head = lax.axis_index("pipe"), lax.axis_index("dp"), lax.axis_index("head")
    n_pipe = lax.axis_size("pipe")
    ahead = (lax.rem(pipe + n_pipe - 1, n_pipe), dp, head)
    behind = (lax.rem(pipe + 1, n_pipe), dp, head)
    is_inner = jnp.logical_or(dp == 1, dp == 2)
    is_end = jnp.logical_not(is_inner)
    low = dp < 2
    my_end = jnp.where(low, 0, 3)
    my_inner = jnp.where(low, 1, 2)
    other_inner = jnp.where(low, 2, 1)
    other_end = jnp.where(low, 3, 0)
    even = lax.rem(pipe, 2) == 0

    def peer(step):
        return (pipe, dp, lax.rem(head + step, HEADS))

    def remote(src, dst, send, recv, device):
        return pltpu.make_async_remote_copy(
            src_ref=src, dst_ref=dst, send_sem=send, recv_sem=recv, device_id=device, device_id_type=MESH
        )

    def load(k, src, dst):
        copy = pltpu.make_async_copy(src, dst, load_sem.at[k])
        copy.start()
        return copy

    plan_in = load(16, plan, planv)
    kg_in = load(0, kg, kgv)
    barrier = pltpu.get_barrier_semaphore()
    greeted = [peer(d) for d in range(1, HEADS)]
    greeted += [(pipe, lax.rem(dp + d, N_DP), head) for d in range(1, N_DP)]
    greeted += [ahead, behind]
    for device in greeted:
        pl.semaphore_signal(barrier, inc=1, device_id=device, device_id_type=MESH)
    act_in = [
        load(1 + 2 * j + m, act.at[m, :, pl.ds(SHARD * j, SHARD)], actv.at[j, pl.ds(ROWS * m, ROWS)])
        for j in range(N_DP)
        for m in range(2)
    ]
    w_in = load(9, w, wv)
    ogv, fp, r1, sp = (oga, ogb), (fpa, fpb), (r1a, r1b), (spa, spb)
    og_in = [
        load(10 + j, og.at[pl.ds(*TOKEN_PARTS[part]), pl.ds(WIDE * half, WIDE)], ogv[part].at[half])
        for j, (part, half) in enumerate(CHUNKS)
    ]
    m1_in = load(14, m1, m1v)
    m2_in = load(15, m2, m2v)

    plan_in.wait()
    kg_in.wait()
    swap = jnp.full((HEAD_COLS, ROWS), planv[0, 0], jnp.int32) != 0
    zero, one = kgv[0].astype(jnp.float32), kgv[1].astype(jnp.float32)
    first = jnp.where(swap, one, zero).astype(jnp.bfloat16)
    kta[head] = first[:, : TOKEN_PARTS[0][1]]
    ktb[head] = first[:, TOKEN_PARTS[0][1] :]
    ktl[head] = jnp.where(swap, zero, one).astype(jnp.bfloat16)
    pl.semaphore_wait(barrier, len(greeted))

    early_parts = (kta, ktb)

    def early_copy(part, d):
        block = early_parts[part].at[head]
        return remote(block, block, key_send.at[part, d - 1], key_recv.at[part, d - 1], peer(d))

    def passed_on(blocks, row, d, via_below):
        if d in (1, 2, 6, 7):
            owner, device = head, peer(d)
        elif d == 3 or (d == 4 and via_below):
            owner, device = lax.rem(head + HEADS - 2, HEADS), peer(d - 2)
        else:
            owner, device = lax.rem(head + 2, HEADS), peer(d + 2)
        block = blocks.at[owner]
        return remote(block, block, key_send.at[row, d - 1], key_recv.at[row, d - 1], device)

    def late_copy(d):
        return passed_on(ktl, 2, d, True)

    def end_key_copy(d):
        return passed_on(ket, 3, d, False)

    far, near = (4, 3, 5, 2, 6, 1, 7), (2, 6, 1, 7)
    for part in range(2):
        for d in far:
            early_copy(part, d).start()
    for copy in act_in:
        copy.wait()

    targets = (other_end, other_inner, my_inner)
    act_copies = [
        remote(actv.at[targets[k]], ab.at[k], act_send.at[k], act_recv.at[k], (pipe, my_inner, head))
        for k in range(3)
    ]
    end_block = remote(kgv, ket.at[head], end_send, end_recv, (pipe, my_inner, head))

    @pl.when(is_end)
    def _():
        end_block.start()
        act_copies[0].start()

    for d in near:
        late_copy(d).start()

    def fp_copy(j):
        part, half = CHUNKS[j]
        return remote(fp[part].at[half], r1[part].at[half], fp_send.at[j], fp_recv.at[j], ahead)

    def sp_copy(j):
        part, half = CHUNKS[j]
        place = out_r.at[pl.ds(*TOKEN_PARTS[part]), pl.ds(WIDE * half, WIDE)]
        return remote(sp[part].at[half], place, sp_send.at[j], sp_recv.at[j], ahead)

    def first(j):
        part, half = CHUNKS[j]
        start, rows = TOKEN_PARTS[part]
        added = nt(early[start : start + rows, :], wv[WIDE * half : WIDE * (half + 1), :])
        fp[part][half] = (ogv[part][half].astype(jnp.float32) + added).astype(jnp.bfloat16)
        fp_copy(j).start()

    w_in.wait()
    for copy in og_in:
        copy.wait()
    for part, (start, rows) in enumerate(TOKEN_PARTS):
        for d in far[::-1]:
            early_copy(part, d).wait_recv()
        early[start : start + rows, :] = early_parts[part][...].reshape(COLS, rows).T
        for j in range(len(CHUNKS)):
            if CHUNKS[j][0] == part:
                first(j)
        if part == 0:

            @pl.when(is_inner)
            def _():
                end_block.wait_recv()
                for d in near:
                    end_key_copy(d).start()

    @pl.when(is_end)
    def _():
        act_copies[1].start()

    late_copy(2).wait_recv()
    late_copy(3).start()
    late_copy(4).start()
    late_copy(6).wait_recv()
    late_copy(5).start()

    @pl.when(is_inner)
    def _():
        end_key_copy(2).wait_recv()
        end_key_copy(3).start()
        end_key_copy(6).wait_recv()
        end_key_copy(4).start()
        end_key_copy(5).start()

    for d in (1, 7, 5, 3, 4):
        late_copy(d).wait_recv()
    late[...] = ktl[...].reshape(COLS, ROWS).T
    swap_all = jnp.full((ROWS, COLS), planv[0, 0], jnp.int32) != 0
    zero, one = early[...].astype(jnp.float32), late[...].astype(jnp.float32)
    kn[:ROWS] = jnp.where(swap_all, one, zero).astype(jnp.bfloat16)
    kn[ROWS:] = jnp.where(swap_all, zero, one).astype(jnp.bfloat16)

    to_end = remote(pb.at[2], ob.at[1], ob_send.at[2], ob_recv.at[1], (pipe, my_end, head))
    to_far = remote(pb.at[0], ob.at[0], ob_send.at[0], ob_recv.at[0], (pipe, other_end, head))
    to_near = remote(pb.at[1], ob.at[0], ob_send.at[1], ob_recv.at[0], (pipe, other_inner, head))

    def second(j):
        part, half = CHUNKS[j]
        start, rows = TOKEN_PARTS[part]
        fp_copy(j).wait_recv()
        added = nt(late[start : start + rows, :], wv[WIDE * half : WIDE * (half + 1), :])
        sp[part][half] = (r1[part][half].astype(jnp.float32) + added).astype(jnp.bfloat16)
        sp_copy(j).start()

    @pl.when(even)
    def _():
        for j in range(len(CHUNKS)):
            second(j)

    @pl.when(is_inner)
    def _():
        pb[2] = tn(actv[my_end], kn[...]).astype(jnp.bfloat16)
        to_end.start()

    @pl.when(is_end)
    def _():
        gf[...] = tn(actv[dp], kn[...])

    def pair(k):
        act_copies[k].wait_recv()
        return own[k] + tn(ab[k], ke[...])

    @pl.when(is_inner)
    def _():
        for k in range(3):
            own[k] = tn(actv[targets[k]], kn[...])
        for d in (1, 7, 3, 5, 4):
            end_key_copy(d).wait_recv()
        for m in range(2):
            for h in range(0, HEADS, 2):
                both = jnp.concatenate([ket[h, m], ket[h + 1, m]], axis=0)
                ke[ROWS * m : ROWS * (m + 1), HEAD_COLS * h : HEAD_COLS * (h + 2)] = both.T
        pb[0] = pair(0).astype(jnp.bfloat16)
        to_far.start()

    @pl.when(jnp.logical_not(even))
    def _():
        for j in range(len(CHUNKS)):
            second(j)

    @pl.when(is_end)
    def _():
        act_copies[1].wait_send()
        act_copies[2].start()

    @pl.when(is_inner)
    def _():
        pb[1] = pair(1).astype(jnp.bfloat16)
        to_near.start()
        gf[...] = pair(2)

    m1_in.wait()
    m2_in.wait()
    to_far.wait_recv()

    @pl.when(is_end)
    def _():
        to_end.wait_recv()
        gf[...] = gf[...] + ob[1].astype(jnp.float32)

    def slab(i, total):
        rows = pl.ds(pl.multiple_of(i * SLAB, SLAB), SLAB)
        gradient = gf[rows, :] + ob[0, rows, :].astype(jnp.float32)
        old_weight = wv[pl.ds(pl.multiple_of(dp * SHARD + i * SLAB, SLAB), SLAB), :].astype(jnp.float32)
        first_fresh = beta_one * m1v[rows, :].astype(jnp.float32) + (1.0 - beta_one) * gradient
        second_fresh = beta_two * m2v[rows, :].astype(jnp.float32) + (1.0 - beta_two) * gradient * gradient
        update = (
            first_fresh / first_fix / (jnp.sqrt(second_fresh / second_fix) + epsilon)
            + weight_decay * old_weight
        )
        owv[rows, :] = (old_weight - learn_rate * update).astype(jnp.bfloat16)
        om1v[rows, :] = first_fresh.astype(jnp.bfloat16)
        om2v[rows, :] = second_fresh.astype(jnp.bfloat16)
        return total + jnp.sum(gradient, axis=0, keepdims=True)

    total = lax.fori_loop(0, SHARD // SLAB, slab, jnp.zeros((1, COLS), jnp.float32))
    ocv[...] = total / SHARD
    stores = [(owv, out_w), (om1v, out_m1), (om2v, out_m2), (ocv, out_c)]
    stores = [pltpu.make_async_copy(src, dst, store_sem.at[k]) for k, (src, dst) in enumerate(stores)]
    for copy in stores:
        copy.start()

    for j in range(len(CHUNKS)):
        sp_copy(j).wait_recv()
    for j in range(len(CHUNKS)):
        fp_copy(j).wait_send()
        sp_copy(j).wait_send()
    for d in far:
        early_copy(0, d).wait_send()
        early_copy(1, d).wait_send()
        late_copy(d).wait_send()

    @pl.when(is_end)
    def _():
        act_copies[0].wait_send()
        act_copies[2].wait_send()
        end_block.wait_send()

    @pl.when(is_inner)
    def _():
        for d in far:
            end_key_copy(d).wait_send()
        to_end.wait_send()
        to_far.wait_send()
        to_near.wait_send()

    for copy in stores:
        copy.wait()


def hand_over(*refs):
    count = (len(refs) - 1) // 2
    sems = refs[-1]
    copies = [pltpu.make_async_copy(refs[k], refs[count + k], sems.at[k]) for k in range(count)]
    for copy in copies:
        copy.start()
    for copy in copies:
        copy.wait()


def body(activations, out_grad, key_grad, key_weight, plan, first_moment, second_moment):
    keys = jnp.swapaxes(key_grad[0], 1, 2)
    bf16, f32 = jnp.bfloat16, jnp.float32
    vmem = pltpu.VMEM
    dma = pltpu.SemaphoreType.DMA
    shard = jax.ShapeDtypeStruct((SHARD, COLS), bf16)
    anywhere = pl.BlockSpec(memory_space=pl.ANY)
    hbm = pl.BlockSpec(memory_space=pltpu.HBM)
    outs = pl.pallas_call(
        kernel,
        out_shape=(
            jax.ShapeDtypeStruct((ROWS, FEAT), bf16),
            shard, shard, shard,
            jax.ShapeDtypeStruct((1, COLS), f32),
        ),
        in_specs=[hbm] * 7,
        out_specs=[anywhere] * 5,
        scratch_shapes=[
            vmem((2, HEAD_COLS, ROWS), bf16),
            vmem((HEADS, HEAD_COLS, TOKEN_PARTS[0][1]), bf16),
            vmem((HEADS, HEAD_COLS, TOKEN_PARTS[1][1]), bf16),
            vmem((HEADS, HEAD_COLS, ROWS), bf16),
            vmem((HEADS, 2, HEAD_COLS, ROWS), bf16),
            vmem((ROWS, COLS), bf16),
            vmem((ROWS, COLS), bf16),
            vmem((2 * ROWS, COLS), bf16),
            vmem((2 * ROWS, COLS), bf16),
            vmem((N_DP, 2 * ROWS, SHARD), bf16),
            vmem((2, TOKEN_PARTS[0][1], WIDE), bf16),
            vmem((2, TOKEN_PARTS[1][1], WIDE), bf16),
            vmem((FEAT, COLS), bf16),
            vmem((SHARD, COLS), bf16),
            vmem((SHARD, COLS), bf16),
            vmem((2, TOKEN_PARTS[0][1], WIDE), bf16),
            vmem((2, TOKEN_PARTS[1][1], WIDE), bf16),
            vmem((2, TOKEN_PARTS[0][1], WIDE), bf16),
            vmem((2, TOKEN_PARTS[1][1], WIDE), bf16),
            vmem((2, TOKEN_PARTS[0][1], WIDE), bf16),
            vmem((2, TOKEN_PARTS[1][1], WIDE), bf16),
            vmem((3, SHARD, COLS), bf16),
            vmem((3, 2 * ROWS, SHARD), bf16),
            vmem((3, SHARD, COLS), f32),
            vmem((2, SHARD, COLS), bf16),
            vmem((SHARD, COLS), f32),
            vmem((SHARD, COLS), bf16),
            vmem((SHARD, COLS), bf16),
            vmem((SHARD, COLS), bf16),
            vmem((1, COLS), f32),
            pltpu.SMEM((1, 2), jnp.int32),
            dma((17,)),
            dma((4, HEADS - 1)), dma((4, HEADS - 1)),
            dma((3,)), dma((3,)),
            dma, dma,
            dma((len(CHUNKS),)), dma((len(CHUNKS),)),
            dma((len(CHUNKS),)), dma((len(CHUNKS),)),
            dma((3,)), dma((2,)),
            dma((4,)),
        ],
        compiler_params=pltpu.CompilerParams(
            collective_id=0, has_side_effects=True, vmem_limit_bytes=40 << 20
        ),
        cost_estimate=pl.CostEstimate(flops=1_400_000_000, bytes_accessed=5_000_000, transcendentals=131_072),
    )(*[pltpu.with_memory_space_constraint(v, pltpu.HBM) for v in (plan, keys, activations[0], out_grad[0], key_weight[0], first_moment[0, 0], second_moment[0, 0])])
    outs = pl.pallas_call(
        hand_over,
        out_shape=tuple(jax.ShapeDtypeStruct(value.shape, value.dtype) for value in outs),
        in_specs=[anywhere] * len(outs),
        out_specs=[hbm] * len(outs),
        scratch_shapes=[dma((len(outs),))],
        compiler_params=pltpu.CompilerParams(vmem_limit_bytes=1 << 20),
    )(*outs)
    passed, new_weight, new_first, new_second, checksum = outs
    return passed[None], new_weight[None, None], new_first[None, None], new_second[None, None], checksum[None, None]


def solution(mesh):
    return jax.shard_map(
        body,
        mesh=mesh,
        in_specs=(
            P("pipe", None, "dp", "head"),
            P("pipe", "dp", "head"),
            P("pipe", None, "dp", "head"),
            P("pipe", "head", None),
            P("pipe", None),
            P("pipe", "head", "dp", None),
            P("pipe", "head", "dp", None),
        ),
        out_specs=(
            P("pipe", "dp", "head"),
            P("pipe", "head", "dp", None),
            P("pipe", "head", "dp", None),
            P("pipe", "head", "dp", None),
            P("pipe", "head", "dp", None),
        ),
        check_vma=False,
    )
```

```python
import functools

import jax
import jax.numpy as jnp
from jax import lax
from jax.experimental import pallas as pl
from jax.experimental.pallas import tpu as pltpu
from jax.sharding import PartitionSpec as P

MESH = pl.DeviceIdType.MESH
beta_one = 0.9
beta_two = 0.95
learn_rate = 0.01
weight_decay = 0.1
epsilon = 1e-08
first_fix = 1.0 - (0.9**10) ** 10
second_fix = 1.0 - (0.95**10) ** 10

HEADS = 8
N_DP = 4
ROWS = 224
COLS = 512
HEAD_COLS = COLS // HEADS
SHARD = 256
FEAT = 1024
TOKEN_PARTS = ((0, 128), (128, 96))
WIDE = 512
CHUNKS = [(part, half) for part in range(2) for half in range(2)]
SLAB = 32


def nt(lhs, rhs):
    return lax.dot_general(lhs, rhs, (((1,), (1,)), ((), ())), preferred_element_type=jnp.float32)


def tn(lhs, rhs):
    return lax.dot_general(lhs, rhs, (((0,), (0,)), ((), ())), preferred_element_type=jnp.float32)


def kernel(
    plan, kg, act, og, w, m1, m2,
    out_r, out_w, out_m1, out_m2, out_c,
    kgv, kta, ktb, ktl, ket, early, late, kn, ke, actv, oga, ogb, wv, m1v, m2v,
    fpa, fpb, r1a, r1b, spa, spb, pb, ab, ob, gf, owv, om1v, om2v, ocv,
    planv, load_sem, key_send, key_recv, act_send, act_recv, end_send, end_recv,
    fp_send, fp_recv, sp_send, sp_recv, ob_send, ob_recv, store_sem,
):
    pipe, dp, head = lax.axis_index("pipe"), lax.axis_index("dp"), lax.axis_index("head")
    n_pipe = lax.axis_size("pipe")
    ahead = (lax.rem(pipe + n_pipe - 1, n_pipe), dp, head)
    behind = (lax.rem(pipe + 1, n_pipe), dp, head)
    is_inner = jnp.logical_or(dp == 1, dp == 2)
    is_end = jnp.logical_not(is_inner)
    low = dp < 2
    my_end = jnp.where(low, 0, 3)
    my_inner = jnp.where(low, 1, 2)
    other_inner = jnp.where(low, 2, 1)
    other_end = jnp.where(low, 3, 0)
    even = lax.rem(pipe, 2) == 0

    def peer(step):
        return (pipe, dp, lax.rem(head + step, HEADS))

    def remote(src, dst, send, recv, device):
        return pltpu.make_async_remote_copy(
            src_ref=src, dst_ref=dst, send_sem=send, recv_sem=recv, device_id=device, device_id_type=MESH
        )

    def load(k, src, dst):
        copy = pltpu.make_async_copy(src, dst, load_sem.at[k])
        copy.start()
        return copy

    plan_in = load(16, plan, planv)
    kg_in = load(0, kg, kgv)
    barrier = pltpu.get_barrier_semaphore()
    greeted = [peer(d) for d in range(1, HEADS)]
    greeted += [(pipe, lax.rem(dp + d, N_DP), head) for d in range(1, N_DP)]
    greeted += [ahead, behind]
    for device in greeted:
        pl.semaphore_signal(barrier, inc=1, device_id=device, device_id_type=MESH)
    act_in = [
        load(1 + 2 * j + m, act.at[m, :, pl.ds(SHARD * j, SHARD)], actv.at[j, pl.ds(ROWS * m, ROWS)])
        for j in range(N_DP)
        for m in range(2)
    ]
    w_in = load(9, w, wv)
    ogv, fp, r1, sp = (oga, ogb), (fpa, fpb), (r1a, r1b), (spa, spb)
    og_in = [
        load(10 + j, og.at[pl.ds(*TOKEN_PARTS[part]), pl.ds(WIDE * half, WIDE)], ogv[part].at[half])
        for j, (part, half) in enumerate(CHUNKS)
    ]
    m1_in = load(14, m1, m1v)
    m2_in = load(15, m2, m2v)

    plan_in.wait()
    kg_in.wait()
    swap = jnp.full((HEAD_COLS, ROWS), planv[0, 0], jnp.int32) != 0
    zero, one = kgv[0].astype(jnp.float32), kgv[1].astype(jnp.float32)
    first = jnp.where(swap, one, zero).astype(jnp.bfloat16)
    kta[head] = first[:, : TOKEN_PARTS[0][1]]
    ktb[head] = first[:, TOKEN_PARTS[0][1] :]
    ktl[head] = jnp.where(swap, zero, one).astype(jnp.bfloat16)
    pl.semaphore_wait(barrier, len(greeted))

    early_parts = (kta, ktb)

    def early_copy(part, d):
        block = early_parts[part].at[head]
        return remote(block, block, key_send.at[part, d - 1], key_recv.at[part, d - 1], peer(d))

    def passed_on(blocks, row, d, via_below):
        if d in (1, 2, 6, 7):
            owner, device = head, peer(d)
        elif d == 3 or (d == 4 and via_below):
            owner, device = lax.rem(head + HEADS - 2, HEADS), peer(d - 2)
        else:
            owner, device = lax.rem(head + 2, HEADS), peer(d + 2)
        block = blocks.at[owner]
        return remote(block, block, key_send.at[row, d - 1], key_recv.at[row, d - 1], device)

    def late_copy(d):
        return passed_on(ktl, 2, d, True)

    def end_key_copy(d):
        return passed_on(ket, 3, d, False)

    far, near = (4, 3, 5, 2, 6, 1, 7), (2, 6, 1, 7)
    for part in range(2):
        for d in far:
            early_copy(part, d).start()
    for copy in act_in:
        copy.wait()

    targets = (other_end, other_inner, my_inner)
    act_copies = [
        remote(actv.at[targets[k]], ab.at[k], act_send.at[k], act_recv.at[k], (pipe, my_inner, head))
        for k in range(3)
    ]
    end_block = remote(kgv, ket.at[head], end_send, end_recv, (pipe, my_inner, head))

    @pl.when(is_end)
    def _():
        end_block.start()
        act_copies[0].start()

    for d in near:
        late_copy(d).start()

    def fp_copy(j):
        part, half = CHUNKS[j]
        return remote(fp[part].at[half], r1[part].at[half], fp_send.at[j], fp_recv.at[j], ahead)

    def sp_copy(j):
        part, half = CHUNKS[j]
        place = out_r.at[pl.ds(*TOKEN_PARTS[part]), pl.ds(WIDE * half, WIDE)]
        return remote(sp[part].at[half], place, sp_send.at[j], sp_recv.at[j], ahead)

    def first(j):
        part, half = CHUNKS[j]
        start, rows = TOKEN_PARTS[part]
        added = nt(early[start : start + rows, :], wv[WIDE * half : WIDE * (half + 1), :])
        fp[part][half] = (ogv[part][half].astype(jnp.float32) + added).astype(jnp.bfloat16)
        fp_copy(j).start()

    w_in.wait()
    for copy in og_in:
        copy.wait()
    for part, (start, rows) in enumerate(TOKEN_PARTS):
        for d in far[::-1]:
            early_copy(part, d).wait_recv()
        early[start : start + rows, :] = early_parts[part][...].reshape(COLS, rows).T
        for j in range(len(CHUNKS)):
            if CHUNKS[j][0] == part:
                first(j)
        if part == 0:

            @pl.when(is_inner)
            def _():
                end_block.wait_recv()
                for d in near:
                    end_key_copy(d).start()

    late_copy(2).wait_recv()
    late_copy(3).start()
    late_copy(4).start()
    late_copy(6).wait_recv()
    late_copy(5).start()

    @pl.when(is_inner)
    def _():
        end_key_copy(2).wait_recv()
        end_key_copy(3).start()
        end_key_copy(6).wait_recv()
        end_key_copy(4).start()
        end_key_copy(5).start()

    for d in (1, 7, 5, 3, 4):
        late_copy(d).wait_recv()
    late[...] = ktl[...].reshape(COLS, ROWS).T
    swap_all = jnp.full((ROWS, COLS), planv[0, 0], jnp.int32) != 0
    zero, one = early[...].astype(jnp.float32), late[...].astype(jnp.float32)
    kn[:ROWS] = jnp.where(swap_all, one, zero).astype(jnp.bfloat16)
    kn[ROWS:] = jnp.where(swap_all, zero, one).astype(jnp.bfloat16)

    to_end = remote(pb.at[2], ob.at[1], ob_send.at[2], ob_recv.at[1], (pipe, my_end, head))
    to_far = remote(pb.at[0], ob.at[0], ob_send.at[0], ob_recv.at[0], (pipe, other_end, head))
    to_near = remote(pb.at[1], ob.at[0], ob_send.at[1], ob_recv.at[0], (pipe, other_inner, head))

    def second(j):
        part, half = CHUNKS[j]
        start, rows = TOKEN_PARTS[part]
        fp_copy(j).wait_recv()
        added = nt(late[start : start + rows, :], wv[WIDE * half : WIDE * (half + 1), :])
        sp[part][half] = (r1[part][half].astype(jnp.float32) + added).astype(jnp.bfloat16)
        sp_copy(j).start()

    @pl.when(is_end)
    def _():
        act_copies[1].start()

    @pl.when(jnp.logical_and(is_end, even))
    def _():
        act_copies[2].start()

    @pl.when(even)
    def _():
        for j in range(len(CHUNKS)):
            second(j)

    @pl.when(is_inner)
    def _():
        pb[2] = tn(actv[my_end], kn[...]).astype(jnp.bfloat16)
        to_end.start()

    @pl.when(is_end)
    def _():
        gf[...] = tn(actv[dp], kn[...])

    def pair(k):
        act_copies[k].wait_recv()
        return tn(actv[targets[k]], kn[...]) + tn(ab[k], ke[...])

    @pl.when(is_inner)
    def _():
        for d in (1, 7, 3, 5, 4):
            end_key_copy(d).wait_recv()
        for m in range(2):
            for h in range(0, HEADS, 2):
                both = jnp.concatenate([ket[h, m], ket[h + 1, m]], axis=0)
                ke[ROWS * m : ROWS * (m + 1), HEAD_COLS * h : HEAD_COLS * (h + 2)] = both.T
        pb[0] = pair(0).astype(jnp.bfloat16)
        to_far.start()

    @pl.when(jnp.logical_not(even))
    def _():
        for j in range(len(CHUNKS)):
            second(j)

    @pl.when(jnp.logical_and(is_end, jnp.logical_not(even)))
    def _():
        act_copies[1].wait_send()
        act_copies[2].start()

    @pl.when(is_inner)
    def _():
        pb[1] = pair(1).astype(jnp.bfloat16)
        to_near.start()
        gf[...] = pair(2)

    m1_in.wait()
    m2_in.wait()
    to_far.wait_recv()

    @pl.when(is_end)
    def _():
        to_end.wait_recv()
        gf[...] = gf[...] + ob[1].astype(jnp.float32)

    def slab(i, total):
        rows = pl.ds(pl.multiple_of(i * SLAB, SLAB), SLAB)
        gradient = gf[rows, :] + ob[0, rows, :].astype(jnp.float32)
        old_weight = wv[pl.ds(pl.multiple_of(dp * SHARD + i * SLAB, SLAB), SLAB), :].astype(jnp.float32)
        first_fresh = beta_one * m1v[rows, :].astype(jnp.float32) + (1.0 - beta_one) * gradient
        second_fresh = beta_two * m2v[rows, :].astype(jnp.float32) + (1.0 - beta_two) * gradient * gradient
        update = (
            first_fresh / first_fix / (jnp.sqrt(second_fresh / second_fix) + epsilon)
            + weight_decay * old_weight
        )
        owv[rows, :] = (old_weight - learn_rate * update).astype(jnp.bfloat16)
        om1v[rows, :] = first_fresh.astype(jnp.bfloat16)
        om2v[rows, :] = second_fresh.astype(jnp.bfloat16)
        return total + jnp.sum(gradient, axis=0, keepdims=True)

    total = lax.fori_loop(0, SHARD // SLAB, slab, jnp.zeros((1, COLS), jnp.float32))
    ocv[...] = total / SHARD
    stores = [(owv, out_w), (om1v, out_m1), (om2v, out_m2), (ocv, out_c)]
    stores = [pltpu.make_async_copy(src, dst, store_sem.at[k]) for k, (src, dst) in enumerate(stores)]
    for copy in stores:
        copy.start()

    for j in range(len(CHUNKS)):
        sp_copy(j).wait_recv()
    for j in range(len(CHUNKS)):
        fp_copy(j).wait_send()
        sp_copy(j).wait_send()
    for d in far:
        early_copy(0, d).wait_send()
        early_copy(1, d).wait_send()
        late_copy(d).wait_send()

    @pl.when(is_end)
    def _():
        act_copies[0].wait_send()

        @pl.when(even)
        def _():
            act_copies[1].wait_send()

        act_copies[2].wait_send()
        end_block.wait_send()

    @pl.when(is_inner)
    def _():
        for d in far:
            end_key_copy(d).wait_send()
        to_end.wait_send()
        to_far.wait_send()
        to_near.wait_send()

    for copy in stores:
        copy.wait()


def hand_over(*refs):
    count = (len(refs) - 1) // 2
    sems = refs[-1]
    copies = [pltpu.make_async_copy(refs[k], refs[count + k], sems.at[k]) for k in range(count)]
    for copy in copies:
        copy.start()
    for copy in copies:
        copy.wait()


def body(activations, out_grad, key_grad, key_weight, plan, first_moment, second_moment):
    keys = jnp.swapaxes(key_grad[0], 1, 2)
    bf16, f32 = jnp.bfloat16, jnp.float32
    vmem = pltpu.VMEM
    dma = pltpu.SemaphoreType.DMA
    shard = jax.ShapeDtypeStruct((SHARD, COLS), bf16)
    anywhere = pl.BlockSpec(memory_space=pl.ANY)
    hbm = pl.BlockSpec(memory_space=pltpu.HBM)
    outs = pl.pallas_call(
        kernel,
        out_shape=(
            jax.ShapeDtypeStruct((ROWS, FEAT), bf16),
            shard, shard, shard,
            jax.ShapeDtypeStruct((1, COLS), f32),
        ),
        in_specs=[hbm] * 7,
        out_specs=[anywhere] * 5,
        scratch_shapes=[
            vmem((2, HEAD_COLS, ROWS), bf16),
            vmem((HEADS, HEAD_COLS, TOKEN_PARTS[0][1]), bf16),
            vmem((HEADS, HEAD_COLS, TOKEN_PARTS[1][1]), bf16),
            vmem((HEADS, HEAD_COLS, ROWS), bf16),
            vmem((HEADS, 2, HEAD_COLS, ROWS), bf16),
            vmem((ROWS, COLS), bf16),
            vmem((ROWS, COLS), bf16),
            vmem((2 * ROWS, COLS), bf16),
            vmem((2 * ROWS, COLS), bf16),
            vmem((N_DP, 2 * ROWS, SHARD), bf16),
            vmem((2, TOKEN_PARTS[0][1], WIDE), bf16),
            vmem((2, TOKEN_PARTS[1][1], WIDE), bf16),
            vmem((FEAT, COLS), bf16),
            vmem((SHARD, COLS), bf16),
            vmem((SHARD, COLS), bf16),
            vmem((2, TOKEN_PARTS[0][1], WIDE), bf16),
            vmem((2, TOKEN_PARTS[1][1], WIDE), bf16),
            vmem((2, TOKEN_PARTS[0][1], WIDE), bf16),
            vmem((2, TOKEN_PARTS[1][1], WIDE), bf16),
            vmem((2, TOKEN_PARTS[0][1], WIDE), bf16),
            vmem((2, TOKEN_PARTS[1][1], WIDE), bf16),
            vmem((3, SHARD, COLS), bf16),
            vmem((3, 2 * ROWS, SHARD), bf16),
            vmem((2, SHARD, COLS), bf16),
            vmem((SHARD, COLS), f32),
            vmem((SHARD, COLS), bf16),
            vmem((SHARD, COLS), bf16),
            vmem((SHARD, COLS), bf16),
            vmem((1, COLS), f32),
            pltpu.SMEM((1, 2), jnp.int32),
            dma((17,)),
            dma((4, HEADS - 1)), dma((4, HEADS - 1)),
            dma((3,)), dma((3,)),
            dma, dma,
            dma((len(CHUNKS),)), dma((len(CHUNKS),)),
            dma((len(CHUNKS),)), dma((len(CHUNKS),)),
            dma((3,)), dma((2,)),
            dma((4,)),
        ],
        compiler_params=pltpu.CompilerParams(
            collective_id=0, has_side_effects=True, vmem_limit_bytes=40 << 20
        ),
        cost_estimate=pl.CostEstimate(flops=1_400_000_000, bytes_accessed=5_000_000, transcendentals=131_072),
    )(*[pltpu.with_memory_space_constraint(v, pltpu.HBM) for v in (plan, keys, activations[0], out_grad[0], key_weight[0], first_moment[0, 0], second_moment[0, 0])])
    outs = pl.pallas_call(
        hand_over,
        out_shape=tuple(jax.ShapeDtypeStruct(value.shape, value.dtype) for value in outs),
        in_specs=[anywhere] * len(outs),
        out_specs=[hbm] * len(outs),
        scratch_shapes=[dma((len(outs),))],
        compiler_params=pltpu.CompilerParams(vmem_limit_bytes=1 << 20),
    )(*outs)
    passed, new_weight, new_first, new_second, checksum = outs
    return passed[None], new_weight[None, None], new_first[None, None], new_second[None, None], checksum[None, None]


def solution(mesh):
    return jax.shard_map(
        body,
        mesh=mesh,
        in_specs=(
            P("pipe", None, "dp", "head"),
            P("pipe", "dp", "head"),
            P("pipe", None, "dp", "head"),
            P("pipe", "head", None),
            P("pipe", None),
            P("pipe", "head", "dp", None),
            P("pipe", "head", "dp", None),
        ),
        out_specs=(
            P("pipe", "dp", "head"),
            P("pipe", "head", "dp", None),
            P("pipe", "head", "dp", None),
            P("pipe", "head", "dp", None),
            P("pipe", "head", "dp", None),
        ),
        check_vma=False,
    )
```
